32 devices in a mesh: ja: 4 (over x, core), ka: 8 (over z, y).
Axes of the slice: x: 2, y: 2, z: 4, core: 2. Of those that a mesh axis runs over, the one named last changes fastest.
Arguments:
- conserved: float32 [5, 128, 64, 128], P(None, 'ja', 'ka'), may hold values from -2 to 6.5, as said below
- blanking: int32 [128, 64, 128], P('ja', 'ka'), may hold values 0 or 1
- wall_type: int32 [128, 128], P('ja'), may hold values from 0 to 2
- char_around: float32 [5, 5], replicated, may hold values from -0.5 to 2.5
- around_to_axial: float32 [5, 5], replicated, may hold values from -0.5 to 2.5
- axial_to_normal: float32 [5, 5], replicated, may hold values from -0.5 to 2.5
- char_back: float32 [5, 5], replicated, may hold values from -0.5 to 2.5
- around_inverse: float32 [5, 128, 128], replicated, may hold values from 0 to 2
- axial_inverse: float32 [5, 128, 128], replicated, may hold values from 0 to 2
- normal_inverse: float32 [5, 64, 64], replicated, may hold values from 0 to 2
Outputs:
- right_side: float32 [5, 128, 64, 128], P(None, 'ja', 'ka')
- update: float32 [5, 128, 64, 128], P(None, 'ja', 'ka')
The draws below stay inside these ranges and needn't reach their ends.
Inputs may be any that keep to these rules, and one draw needn't show every extreme that they name: `conserved`: component 0, the density, is 0.5 or more in every cell.
All inputs are finite; a program needn't handle non-finite values. No bound on the sum of `blanking` on one device may be relied on, other than what follows from the above.
Results may differ from the reference program's by a relative error of at most 0.00019.
Values sent between devices are 32-bit elements; how exact they have to be, the bound alone decides.
A program may use at most 64 MiB of HBM per device.

```python
import math
import jax
import jax.numpy as jnp
from jax import lax

NI = 128
CJ = 32
CK = 8
NJ = 128
NK = 64


def draw_conserved(key, part):
    key = jax.random.fold_in(key, 1)
    first_key, second_key, third_key = jax.random.split(key, 3)
    shape = (NJ, NK, NI)
    density = jax.random.uniform(first_key, shape, jnp.float32, 0.6, 1.6)
    velocity = jax.random.uniform(second_key, (3,) + shape, jnp.float32, -0.6, 0.6)
    pressure = jax.random.uniform(third_key, shape, jnp.float32, 0.6, 1.4)
    momentum = density[None] * velocity
    energy = pressure / 0.4 + 0.5 * density * jnp.sum(velocity * velocity, axis=0)
    return jnp.concatenate([density[None], momentum, energy[None]], axis=0)


def small_matrix(key):
    return 2.0 * jnp.eye(5, dtype=jnp.float32) + jax.random.uniform(key, (5, 5), jnp.float32, -0.45, 0.45)


def draw_char_around(key, part):
    key = jax.random.fold_in(key, 11)
    return small_matrix(key)


def draw_around_to_axial(key, part):
    key = jax.random.fold_in(key, 12)
    return small_matrix(key)


def draw_axial_to_normal(key, part):
    key = jax.random.fold_in(key, 13)
    return small_matrix(key)


def draw_char_back(key, part):
    key = jax.random.fold_in(key, 14)
    return small_matrix(key)


def line_inverse(key, count, cells, shortest, longest, rough_low, rough_high):
    length_key, rough_key = jax.random.split(key, 2)
    lengths = cells * jnp.exp(jax.random.uniform(length_key, (2, 5, 1, 1), jnp.float32, math.log(shortest), math.log(longest)))
    places = jnp.arange(count).astype(jnp.float32)
    offset = places[:, None] - places[None, :]
    spread = jnp.abs(offset)[None]
    kernel = jnp.where(offset[None] >= 0, jnp.exp(-spread / lengths[0]), jnp.exp(-spread / lengths[1]))
    rough = jax.random.uniform(rough_key, (5, count, count), jnp.float32, rough_low, rough_high)
    return jnp.eye(count, dtype=jnp.float32)[None] + 1.5 * rough * kernel / (lengths[0] + lengths[1])


def draw_around_inverse(key, part):
    key = jax.random.fold_in(key, 21)
    return line_inverse(key, NI, NI // 8, 1.5, 6.0, 0.5, 1.5)


def draw_axial_inverse(key, part):
    key = jax.random.fold_in(key, 22)
    return line_inverse(key, NJ, CJ, 1.5, 6.0, 0.5, 1.5)


def draw_normal_inverse(key, part):
    key = jax.random.fold_in(key, 23)
    return line_inverse(key, NK, CK, 1.5, 6.0, 0.5, 1.5)


def with_ends(values, rng, least, high):
    spot = [jax.random.randint(jax.random.fold_in(rng, axis), (), 0, length) for axis, length in enumerate(values.shape)]
    main_axis = values.shape.index(max(values.shape))
    next_to = spot[:main_axis] + [(spot[main_axis] + 1) % values.shape[main_axis]] + spot[main_axis + 1:]
    return values.at[tuple(spot)].set(least).at[tuple(next_to)].set(high)


def setup_inputs(seed: int = 0) -> dict:
    keys = jax.random.split(jax.random.key(seed), 11)
    conserved = draw_conserved(jax.random.fold_in(keys[10], 71), 0)
    blanking = with_ends((jax.random.randint(keys[1], (NJ, NK, NI), 0, 10) < 9).astype(jnp.int32), jax.random.fold_in(keys[1], 1), 0, 1)
    wall_type = with_ends(jax.random.randint(keys[2], (NJ, NI), 0, 3), jax.random.fold_in(keys[2], 1), 0, 2).astype(jnp.int32)
    char_around = draw_char_around(jax.random.fold_in(keys[10], 71), 0)
    around_to_axial = draw_around_to_axial(jax.random.fold_in(keys[10], 71), 0)
    axial_to_normal = draw_axial_to_normal(jax.random.fold_in(keys[10], 71), 0)
    char_back = draw_char_back(jax.random.fold_in(keys[10], 71), 0)
    around_inverse = draw_around_inverse(jax.random.fold_in(keys[10], 71), 0)
    axial_inverse = draw_axial_inverse(jax.random.fold_in(keys[10], 71), 0)
    normal_inverse = draw_normal_inverse(jax.random.fold_in(keys[10], 71), 0)
    return {"conserved": conserved, "blanking": blanking, "wall_type": wall_type, "char_around": char_around, "around_to_axial": around_to_axial, "axial_to_normal": axial_to_normal, "char_back": char_back, "around_inverse": around_inverse, "axial_inverse": axial_inverse, "normal_inverse": normal_inverse}


HIGHEST = lax.Precision.HIGHEST
FREESTREAM = (1.0, 0.4, 0.1, 0.0, 2.585)


def freestream(like):
    return jnp.array(FREESTREAM, like.dtype).reshape(5, 1, 1, 1)


def flux_along(state, direction):
    density = state[0]
    velocity = state[direction] / density
    kinetic = state[1] * state[1] + state[2] * state[2] + state[3] * state[3]
    pressure = 0.4 * (state[4] - 0.5 * kinetic / density)
    pieces = [state[direction]]
    for member in (1, 2, 3):
        addend = state[member] * velocity
        if member == direction:
            addend = addend + pressure
        pieces.append(addend)
    pieces.append((state[4] + pressure) * velocity)
    return jnp.stack(pieces)


def wall_ghost(first_layer, second_layer, wall_type):
    negate = jnp.array([1.0, 1.0, 1.0, -1.0, 1.0], first_layer.dtype).reshape(5, 1, 1)
    mirror = jnp.stack([second_layer * negate, first_layer * negate], axis=2)
    extend = jnp.stack([first_layer, first_layer], axis=2)
    outer = jnp.broadcast_to(freestream(first_layer), mirror.shape)
    kind = wall_type[None, :, None, :]
    return jnp.where(kind == 0, mirror, jnp.where(kind == 1, extend, outer))


def damping(reader):
    second_diff = reader(1) - 2.0 * reader(0) + reader(-1)
    fourth_diff = reader(2) - 4.0 * reader(1) + 6.0 * reader(0) - 4.0 * reader(-1) + reader(-2)
    return -0.25 * second_diff + fourth_diff / 32.0


def balance(padded):
    width_j = padded.shape[1] - 4
    width_k = padded.shape[2] - 4
    inner = padded[:, 2:-2, 2:-2, :]

    def around_at(offset):
        return jnp.roll(inner, -offset, axis=3)

    flux_i = flux_along(inner, 1)
    total = 0.5 * (jnp.roll(flux_i, -1, axis=3) - jnp.roll(flux_i, 1, axis=3)) + damping(around_at)
    column = padded[:, :, 2:-2, :]
    flux_j = flux_along(column, 2)

    def axial_at(offset):
        return column[:, 2 + offset:2 + offset + width_j]

    total = total + 0.5 * (flux_j[:, 3:3 + width_j] - flux_j[:, 1:1 + width_j]) + damping(axial_at)
    slab = padded[:, 2:-2, :, :]
    flux_k = flux_along(slab, 3)

    def normal_at(offset):
        return slab[:, :, 2 + offset:2 + offset + width_k]

    total = total + 0.5 * (flux_k[:, :, 3:3 + width_k] - flux_k[:, :, 1:1 + width_k]) + damping(normal_at)
    return total


def reference(conserved, blanking, wall_type, char_around, around_to_axial, axial_to_normal, char_back, around_inverse, axial_inverse, normal_inverse):
    count_j = conserved.shape[1]
    count_k = conserved.shape[2]
    count_i = conserved.shape[3]
    padded = jnp.broadcast_to(freestream(conserved), (5, count_j + 4, count_k + 4, count_i))
    padded = padded.at[:, 2:-2, 2:-2, :].set(conserved)
    ghost = wall_ghost(conserved[:, :, 0], conserved[:, :, 1], wall_type)
    padded = padded.at[:, 2:-2, 0:2, :].set(ghost)
    weight = blanking.astype(conserved.dtype)
    right_side = -0.5 * balance(padded) * weight
    mixed = jnp.einsum('ab,bjki->ajki', char_around, right_side, precision=HIGHEST)
    mixed = jnp.einsum('lab,ljkb->ljka', around_inverse, mixed, precision=HIGHEST)
    mixed = jnp.einsum('ab,bjki->ajki', around_to_axial, mixed, precision=HIGHEST)
    mixed = jnp.einsum('lab,lbki->laki', axial_inverse, mixed, precision=HIGHEST)
    mixed = jnp.einsum('ab,bjki->ajki', axial_to_normal, mixed, precision=HIGHEST)
    mixed = jnp.einsum('lab,ljbi->ljai', normal_inverse, mixed, precision=HIGHEST)
    update = jnp.einsum('ab,bjki->ajki', char_back, mixed, precision=HIGHEST) * weight
    return right_side, update
```

```python
import functools

import jax
import jax.numpy as jnp
from jax import lax
from jax.experimental import pallas as pl
from jax.experimental.pallas import tpu as pltpu
from jax.sharding import PartitionSpec as P

F32 = jnp.float32
BF16 = jnp.bfloat16
MESH = pl.DeviceIdType.MESH
FREESTREAM = (1.0, 0.4, 0.1, 0.0, 2.585)
TOP = 8


def flux(state, direction):
    inverse = 1.0 / state[0]
    kinetic = state[1] * state[1] + state[2] * state[2] + state[3] * state[3]
    pressure = 0.4 * (state[4] - 0.5 * kinetic * inverse)
    velocity = state[direction] * inverse
    pieces = [state[direction]]
    for member in (1, 2, 3):
        piece = state[member] * velocity
        pieces.append(piece + pressure if member == direction else piece)
    pieces.append((state[4] + pressure) * velocity)
    return pieces


def mix(matrix, values):
    out = []
    for a in range(5):
        total = matrix[a, 0] * values[0]
        for b in range(1, 5):
            total = total + matrix[a, b] * values[b]
        out.append(total)
    return out


def halves(x):
    high = x.astype(BF16)
    return high, (x - high.astype(F32)).astype(BF16)


def dot(x, y, dims):
    return lax.dot_general(x, y, (dims, ((), ())), preferred_element_type=F32)


def kernel(
    nja,
    nka,
    cells,
    blanking,
    wall,
    char_around,
    around_to_axial,
    axial_to_normal,
    char_back,
    around_inverse,
    axial_inverse,
    normal_inverse,
    right_side,
    update,
    q,
    jhalo,
    first,
    asend,
    x,
    solved,
    bsend,
    y,
    w,
    z,
    normal,
    csend,
    u,
    around3,
    axial3,
    normal3,
    jsem,
    ksem,
    a_send,
    a_recv,
    b_send,
    b_recv,
    w_send,
    w_recv,
    c_send,
    c_recv,
):
    cj = wall.shape[0]
    ck = cells.shape[1] // cj
    ni = cells.shape[2]
    kp = ck // nja
    jq = cj // nka
    mj = lax.axis_index("ja")
    mk = lax.axis_index("ka")

    barrier = pltpu.get_barrier_semaphore()
    for o in range(1, nja):
        pl.semaphore_signal(
            barrier, inc=1, device_id={"ja": lax.rem(mj + o, nja)}, device_id_type=MESH
        )
    for o in range(1, nka):
        pl.semaphore_signal(
            barrier, inc=1, device_id={"ka": lax.rem(mk + o, nka)}, device_id_type=MESH
        )

    def spread(k, carry):
        for c in range(5):
            q[c, k + 2, TOP : TOP + cj, :] = cells[c, pl.ds(k, cj, stride=ck), :]
        return carry

    lax.fori_loop(0, ck, spread, 0)
    pl.semaphore_wait(barrier, nja - 1 + nka - 1)

    def khalo(upward):
        if upward:
            src, dst, other = ck, 0, mk + 1
        else:
            src, dst, other = 2, ck + 2, mk - 1
        return pltpu.make_async_remote_copy(
            src_ref=q.at[:, src : src + 2, TOP : TOP + cj, :],
            dst_ref=q.at[:, dst : dst + 2, TOP : TOP + cj, :],
            send_sem=ksem.at[0, int(upward)],
            recv_sem=ksem.at[1, int(upward)],
            device_id={"ka": other},
            device_id_type=MESH,
        )

    def jhalo_copy(upward):
        if upward:
            src, dst, other = (cj - 2) * ck, 0, mj + 1
        else:
            src, dst, other = 0, 1, mj - 1
        return pltpu.make_async_remote_copy(
            src_ref=cells.at[:, src : src + 2 * ck, :],
            dst_ref=jhalo.at[dst],
            send_sem=jsem.at[0, int(upward)],
            recv_sem=jsem.at[1, int(upward)],
            device_id={"ja": other},
            device_id_type=MESH,
        )

    @pl.when(mj < nja - 1)
    def _():
        jhalo_copy(True).start()

    @pl.when(mj > 0)
    def _():
        jhalo_copy(False).start()

    @pl.when(mk < nka - 1)
    def _():
        khalo(True).start()

    @pl.when(mk > 0)
    def _():
        khalo(False).start()

    @pl.when(mj == 0)
    def _():
        for c in range(5):
            jhalo[0, c] = jnp.full((2 * ck, ni), FREESTREAM[c], F32)

    @pl.when(mj == nja - 1)
    def _():
        for c in range(5):
            jhalo[1, c] = jnp.full((2 * ck, ni), FREESTREAM[c], F32)

    @pl.when(mk == 0)
    def _():
        kind = wall[...]
        for c in range(5):
            near = q[c, 2, TOP : TOP + cj, :]
            far = q[c, 3, TOP : TOP + cj, :]
            sign = -1.0 if c == 3 else 1.0
            rest = jnp.where(kind == 1, near, FREESTREAM[c])
            q[c, 1, TOP : TOP + cj, :] = jnp.where(kind == 0, sign * near, rest)
            q[c, 0, TOP : TOP + cj, :] = jnp.where(kind == 0, sign * far, rest)

    @pl.when(mk == nka - 1)
    def _():
        for c in range(5):
            for r in range(2):
                q[c, ck + 2 + r, TOP : TOP + cj, :] = jnp.full((cj, ni), FREESTREAM[c], F32)

    for c in range(5):
        high, low = halves(around_inverse[c])
        around3[c] = jnp.concatenate([high, low, high], axis=1)
        high, low = halves(axial_inverse[c])
        axial3[c] = jnp.concatenate([high, high, low], axis=1)
        high, low = halves(normal_inverse[c])
        normal3[c] = jnp.concatenate([high, high, low], axis=1)

    @pl.when(mj > 0)
    def _():
        jhalo_copy(True).wait_recv()

    @pl.when(mj < nja - 1)
    def _():
        jhalo_copy(False).wait_recv()

    def plane(k, carry):
        at = k + 2
        for c in range(5):
            for r in range(2):
                row = pl.ds(r * ck + k, 1)
                q[c, at, TOP - 2 + r : TOP - 1 + r, :] = jhalo[0, c, row, :]
                q[c, at, TOP + cj + r : TOP + cj + r + 1, :] = jhalo[1, c, row, :]

        def rows(offset):
            return [q[c, at, TOP + offset : TOP + offset + cj, :] for c in range(5)]

        def layer(offset):
            return [q[c, at + offset, TOP : TOP + cj, :] for c in range(5)]

        here = rows(0)
        flow = flux(here, 1)
        total = []
        for c in range(5):
            plus = 0.5 * flow[c] - 0.375 * here[c]
            minus = -0.5 * flow[c] - 0.375 * here[c]
            wide = pltpu.roll(here[c], 2, 1) + pltpu.roll(here[c], ni - 2, 1)
            total.append(
                2.0625 * here[c]
                + pltpu.roll(plus, ni - 1, 1)
                + pltpu.roll(minus, 1, 1)
                + wide * (1.0 / 32.0)
            )
        for direction, reader in ((2, rows), (3, layer)):
            above, below = reader(1), reader(-1)
            top, bottom = flux(above, direction), flux(below, direction)
            for c in range(5):
                total[c] = total[c] + 0.5 * (top[c] - bottom[c]) - 0.375 * (above[c] + below[c])
            above, below = reader(2), reader(-2)
            for c in range(5):
                total[c] = total[c] + (above[c] + below[c]) * (1.0 / 32.0)
        weight = -0.5 * blanking[pl.ds(k, cj, stride=ck), :].astype(F32)
        total = [t * weight for t in total]
        for c in range(5):
            right_side[c, pl.ds(k, cj, stride=ck), :] = total[c]
        mixed = mix(char_around, total)
        for c in range(5):
            first[c, k] = mixed[c]
        return carry

    def a_copy(dest):
        return pltpu.make_async_remote_copy(
            src_ref=asend.at[dest],
            dst_ref=x.at[:, :, pl.ds(pl.multiple_of(mj * cj, 8), cj), :],
            send_sem=a_send.at[dest],
            recv_sem=a_recv.at[mj],
            device_id={"ja": dest},
            device_id_type=MESH,
        )

    def around(start, count):
        out = []
        for c in range(5):
            high, low = halves(first[c, start : start + count].reshape(count * cj, ni))
            out.append(
                dot(jnp.concatenate([high, high, low], axis=1), around3[c], ((1,), (1,)))
            )
        out = mix(around_to_axial, out)
        for c in range(5):
            for s in range(count):
                k = start + s
                asend[k // kp, c, k % kp] = out[c][s * cj : (s + 1) * cj]
        for dest in range(start // kp, (start + count) // kp):

            @pl.when(dest != mj)
            def _():
                a_copy(dest).start()

    edge = 2
    lax.fori_loop(edge, ck - edge, plane, 0)
    around(edge, ck - 2 * edge)

    @pl.when(mk > 0)
    def _():
        khalo(True).wait_recv()

    @pl.when(mk < nka - 1)
    def _():
        khalo(False).wait_recv()

    lax.fori_loop(0, edge, plane, 0)
    around(0, edge)
    lax.fori_loop(ck - edge, ck, plane, 0)
    around(ck - edge, edge)

    own = pl.ds(pl.multiple_of(mj * cj, 8), cj)
    for c in range(5):
        for s in range(kp):
            x[c, s, own, :] = asend[mj, c, s]

    for o in range(1, nja):
        source = lax.rem(mj + o, nja)
        pltpu.make_async_remote_copy(
            src_ref=asend.at[source],
            dst_ref=x.at[:, :, pl.ds(pl.multiple_of(source * cj, 8), cj), :],
            send_sem=a_send.at[source],
            recv_sem=a_recv.at[source],
            device_id={"ja": source},
            device_id_type=MESH,
        ).wait_recv()

    for c in range(5):
        high, low = halves(jnp.concatenate([x[c, s] for s in range(kp)], axis=1))
        out = dot(axial3[c], jnp.concatenate([high, low, high], axis=0), ((1,), (0,)))
        for s in range(kp):
            solved[c, s] = out[:, s * ni : (s + 1) * ni]

    def b_copy(dest, source):
        return pltpu.make_async_remote_copy(
            src_ref=bsend.at[dest],
            dst_ref=y.at[:, pl.ds(pl.multiple_of(source * (kp * cj), 8), kp * cj), :],
            send_sem=b_send.at[dest],
            recv_sem=b_recv.at[source],
            device_id={"ja": dest},
            device_id_type=MESH,
        )

    for o in range(1, nja + 1):
        dest = lax.rem(mj + o, nja)
        for s in range(kp):
            block = [
                solved[c, s, pl.ds(pl.multiple_of(dest * cj, 8), cj), :] for c in range(5)
            ]
            block = mix(axial_to_normal, block)
            for c in range(5):
                if o < nja:
                    bsend[dest, c, s * cj : (s + 1) * cj, :] = block[c]
                else:
                    y[c, pl.ds(pl.multiple_of((mj * kp + s) * cj, 8), cj), :] = block[c]
        if o < nja:
            b_copy(dest, mj).start()
    for o in range(1, nja):
        source = lax.rem(mj + o, nja)
        b_copy(source, source).wait_recv()

    def w_copy(dest, source):
        return pltpu.make_async_remote_copy(
            src_ref=w.at[dest],
            dst_ref=z.at[:, :, pl.ds(pl.multiple_of(source * ck, 8), ck), :],
            send_sem=w_send.at[dest],
            recv_sem=w_recv.at[source],
            device_id={"ka": dest},
            device_id_type=MESH,
        )

    for o in range(1, nka + 1):
        dest = lax.rem(mk + o, nka)
        for s in range(jq):
            for c in range(5):
                tile = y[c, pl.ds(dest * jq + s, ck, stride=cj), :]
                if o < nka:
                    w[dest, c, s] = tile
                else:
                    z[c, s, pl.ds(pl.multiple_of(mk * ck, 8), ck), :] = tile
        if o < nka:
            w_copy(dest, mk).start()
    for o in range(1, nka):
        source = lax.rem(mk + o, nka)
        w_copy(source, source).wait_recv()

    for c in range(5):
        high, low = halves(jnp.concatenate([z[c, s] for s in range(jq)], axis=1))
        out = dot(normal3[c], jnp.concatenate([high, low, high], axis=0), ((1,), (0,)))
        for s in range(jq):
            normal[c, s] = out[:, s * ni : (s + 1) * ni]

    def c_copy(dest, source):
        return pltpu.make_async_remote_copy(
            src_ref=csend.at[dest],
            dst_ref=u.at[:, pl.ds(pl.multiple_of(source * (jq * ck), 8), jq * ck), :],
            send_sem=c_send.at[dest],
            recv_sem=c_recv.at[source],
            device_id={"ka": dest},
            device_id_type=MESH,
        )

    for o in range(1, nka + 1):
        dest = lax.rem(mk + o, nka)
        for s in range(jq):
            block = [
                normal[c, s, pl.ds(pl.multiple_of(dest * ck, 8), ck), :] for c in range(5)
            ]
            block = mix(char_back, block)
            for c in range(5):
                if o < nka:
                    csend[dest, c, s * ck : (s + 1) * ck, :] = block[c]
                else:
                    u[c, pl.ds(pl.multiple_of((mk * jq + s) * ck, 8), ck), :] = block[c]
        if o < nka:
            c_copy(dest, mk).start()
    for o in range(1, nka):
        source = lax.rem(mk + o, nka)
        c_copy(source, source).wait_recv()

    weight = blanking[...].astype(F32)
    for c in range(5):
        update[c] = u[c] * weight

    for upward, last, here in ((True, nja - 1, mj), (False, 0, mj)):

        @pl.when(here != last)
        def _(upward=upward):
            jhalo_copy(upward).wait_send()

    for upward, last, here in ((True, nka - 1, mk), (False, 0, mk)):

        @pl.when(here != last)
        def _(upward=upward):
            khalo(upward).wait_send()

    for o in range(1, nja):
        other = lax.rem(mj + o, nja)
        a_copy(other).wait_send()
        b_copy(other, mj).wait_send()
    for o in range(1, nka):
        other = lax.rem(mk + o, nka)
        w_copy(other, mk).wait_send()
        c_copy(other, mk).wait_send()


def body(
    conserved,
    blanking,
    wall_type,
    char_around,
    around_to_axial,
    axial_to_normal,
    char_back,
    around_inverse,
    axial_inverse,
    normal_inverse,
):
    nja = lax.axis_size("ja")
    nka = lax.axis_size("ka")
    _, cj, ck, ni = conserved.shape
    nj, nk = cj * nja, ck * nka
    kp, jq = ck // nja, cj // nka
    vmem = pl.BlockSpec(memory_space=pltpu.VMEM)
    smem = pl.BlockSpec(memory_space=pltpu.SMEM)
    flat = jax.ShapeDtypeStruct((5, cj * ck, ni), F32)
    dma = pltpu.SemaphoreType.DMA
    right_side, update = pl.pallas_call(
        functools.partial(kernel, nja, nka),
        out_shape=(flat, flat),
        in_specs=[vmem] * 3 + [smem] * 4 + [vmem] * 3,
        out_specs=(vmem, vmem),
        scratch_shapes=[
            pltpu.VMEM((5, ck + 4, cj + 16, ni), F32),
            pltpu.VMEM((2, 5, 2 * ck, ni), F32),
            pltpu.VMEM((5, ck, cj, ni), F32),
            pltpu.VMEM((nja, 5, kp, cj, ni), F32),
            pltpu.VMEM((5, kp, nj, ni), F32),
            pltpu.VMEM((5, kp, nj, ni), F32),
            pltpu.VMEM((nja, 5, kp * cj, ni), F32),
            pltpu.VMEM((5, ck * cj, ni), F32),
            pltpu.VMEM((nka, 5, jq, ck, ni), F32),
            pltpu.VMEM((5, jq, nk, ni), F32),
            pltpu.VMEM((5, jq, nk, ni), F32),
            pltpu.VMEM((nka, 5, jq * ck, ni), F32),
            pltpu.VMEM((5, cj * ck, ni), F32),
            pltpu.VMEM((5, ni, 3 * ni), BF16),
            pltpu.VMEM((5, nj, 3 * nj), BF16),
            pltpu.VMEM((5, nk, 3 * nk), BF16),
            dma((2, 2)),
            dma((2, 2)),
            dma((nja,)),
            dma((nja,)),
            dma((nja,)),
            dma((nja,)),
            dma((nka,)),
            dma((nka,)),
            dma((nka,)),
            dma((nka,)),
        ],
        compiler_params=pltpu.CompilerParams(
            collective_id=0, has_side_effects=True, vmem_limit_bytes=48 * 1024 * 1024
        ),
    )(
        conserved.reshape(5, cj * ck, ni),
        blanking.reshape(cj * ck, ni),
        wall_type,
        char_around,
        around_to_axial,
        axial_to_normal,
        char_back,
        around_inverse,
        axial_inverse,
        normal_inverse,
    )
    return right_side.reshape(conserved.shape), update.reshape(conserved.shape)


def solution(mesh):
    slabs = P(None, "ja", "ka", None)
    return jax.shard_map(
        body,
        mesh=mesh,
        in_specs=(slabs, P("ja", "ka", None), P("ja", None)) + (P(),) * 7,
        out_specs=(slabs, slabs),
        check_vma=False,
    )
```

```python
import functools

import jax
import jax.numpy as jnp
from jax import lax
from jax.experimental import pallas as pl
from jax.experimental.pallas import tpu as pltpu
from jax.sharding import PartitionSpec as P

F32 = jnp.float32
BF16 = jnp.bfloat16
MESH = pl.DeviceIdType.MESH
FREESTREAM = (1.0, 0.4, 0.1, 0.0, 2.585)
TOP = 8


def flux(state, direction):
    inverse = 1.0 / state[0]
    kinetic = state[1] * state[1] + state[2] * state[2] + state[3] * state[3]
    pressure = 0.4 * (state[4] - 0.5 * kinetic * inverse)
    velocity = state[direction] * inverse
    pieces = [state[direction]]
    for member in (1, 2, 3):
        piece = state[member] * velocity
        pieces.append(piece + pressure if member == direction else piece)
    pieces.append((state[4] + pressure) * velocity)
    return pieces


def mix(matrix, values):
    out = []
    for a in range(5):
        total = matrix[a, 0] * values[0]
        for b in range(1, 5):
            total = total + matrix[a, b] * values[b]
        out.append(total)
    return out


def halves(x):
    high = x.astype(BF16)
    return high, (x - high.astype(F32)).astype(BF16)


def dot(x, y, dims):
    return lax.dot_general(x, y, (dims, ((), ())), preferred_element_type=F32)


def kernel(
    nja,
    nka,
    *refs,
):
    sources, refs = refs[:10], refs[10:]
    right_side, update = refs[:2]
    inputs, refs = refs[2:12], refs[12:]
    (
        cells,
        blanking,
        wall,
        char_around,
        around_to_axial,
        axial_to_normal,
        char_back,
        around_inverse,
        axial_inverse,
        normal_inverse,
    ) = inputs
    (
    q,
    jhalo,
    first,
    asend,
    x,
    solved,
    bsend,
    y,
    w,
    z,
    normal,
    csend,
    u,
    around3,
    axial3,
    normal3,
    jsem,
    ksem,
    a_send,
    a_recv,
    b_send,
    b_recv,
    w_send,
    w_recv,
    c_send,
    c_recv,
        insem,
    ) = refs
    loads = [
        pltpu.make_async_copy(source, held, insem.at[n])
        for n, (source, held) in enumerate(zip(sources, inputs))
    ]
    for load in loads:
        load.start()
    cj = wall.shape[0]
    ck = cells.shape[1] // cj
    ni = cells.shape[2]
    kp = ck // nja
    jq = cj // nka
    mj = lax.axis_index("ja")
    mk = lax.axis_index("ka")

    barrier = pltpu.get_barrier_semaphore()
    for o in range(1, nja):
        pl.semaphore_signal(
            barrier, inc=1, device_id={"ja": lax.rem(mj + o, nja)}, device_id_type=MESH
        )
    for o in range(1, nka):
        pl.semaphore_signal(
            barrier, inc=1, device_id={"ka": lax.rem(mk + o, nka)}, device_id_type=MESH
        )

    loads[0].wait()

    def spread(k, carry):
        for c in range(5):
            q[c, k + 2, TOP : TOP + cj, :] = cells[c, pl.ds(k, cj, stride=ck), :]
        return carry

    lax.fori_loop(0, ck, spread, 0)
    pl.semaphore_wait(barrier, nja - 1 + nka - 1)

    def khalo(upward):
        if upward:
            src, dst, other = ck, 0, mk + 1
        else:
            src, dst, other = 2, ck + 2, mk - 1
        return pltpu.make_async_remote_copy(
            src_ref=q.at[:, src : src + 2, TOP : TOP + cj, :],
            dst_ref=q.at[:, dst : dst + 2, TOP : TOP + cj, :],
            send_sem=ksem.at[0, int(upward)],
            recv_sem=ksem.at[1, int(upward)],
            device_id={"ka": other},
            device_id_type=MESH,
        )

    def jhalo_copy(upward):
        if upward:
            src, dst, other = (cj - 2) * ck, 0, mj + 1
        else:
            src, dst, other = 0, 1, mj - 1
        return pltpu.make_async_remote_copy(
            src_ref=cells.at[:, src : src + 2 * ck, :],
            dst_ref=jhalo.at[dst],
            send_sem=jsem.at[0, int(upward)],
            recv_sem=jsem.at[1, int(upward)],
            device_id={"ja": other},
            device_id_type=MESH,
        )

    @pl.when(mj < nja - 1)
    def _():
        jhalo_copy(True).start()

    @pl.when(mj > 0)
    def _():
        jhalo_copy(False).start()

    @pl.when(mk < nka - 1)
    def _():
        khalo(True).start()

    @pl.when(mk > 0)
    def _():
        khalo(False).start()

    for load in loads[1:]:
        load.wait()

    @pl.when(mj == 0)
    def _():
        for c in range(5):
            jhalo[0, c] = jnp.full((2 * ck, ni), FREESTREAM[c], F32)

    @pl.when(mj == nja - 1)
    def _():
        for c in range(5):
            jhalo[1, c] = jnp.full((2 * ck, ni), FREESTREAM[c], F32)

    @pl.when(mk == 0)
    def _():
        kind = wall[...]
        for c in range(5):
            near = q[c, 2, TOP : TOP + cj, :]
            far = q[c, 3, TOP : TOP + cj, :]
            sign = -1.0 if c == 3 else 1.0
            rest = jnp.where(kind == 1, near, FREESTREAM[c])
            q[c, 1, TOP : TOP + cj, :] = jnp.where(kind == 0, sign * near, rest)
            q[c, 0, TOP : TOP + cj, :] = jnp.where(kind == 0, sign * far, rest)

    @pl.when(mk == nka - 1)
    def _():
        for c in range(5):
            for r in range(2):
                q[c, ck + 2 + r, TOP : TOP + cj, :] = jnp.full((cj, ni), FREESTREAM[c], F32)

    for c in range(5):
        high, low = halves(around_inverse[c])
        around3[c] = jnp.concatenate([high, low, high], axis=1)
        high, low = halves(axial_inverse[c])
        axial3[c] = jnp.concatenate([high, high, low], axis=1)
        high, low = halves(normal_inverse[c])
        normal3[c] = jnp.concatenate([high, high, low], axis=1)

    @pl.when(mj > 0)
    def _():
        jhalo_copy(True).wait_recv()

    @pl.when(mj < nja - 1)
    def _():
        jhalo_copy(False).wait_recv()

    def plane(k, carry):
        at = k + 2
        for c in range(5):
            for r in range(2):
                row = pl.ds(r * ck + k, 1)
                q[c, at, TOP - 2 + r : TOP - 1 + r, :] = jhalo[0, c, row, :]
                q[c, at, TOP + cj + r : TOP + cj + r + 1, :] = jhalo[1, c, row, :]

        def rows(offset):
            return [q[c, at, TOP + offset : TOP + offset + cj, :] for c in range(5)]

        def layer(offset):
            return [q[c, at + offset, TOP : TOP + cj, :] for c in range(5)]

        here = rows(0)
        flow = flux(here, 1)
        total = []
        for c in range(5):
            plus = 0.5 * flow[c] - 0.375 * here[c]
            minus = -0.5 * flow[c] - 0.375 * here[c]
            wide = pltpu.roll(here[c], 2, 1) + pltpu.roll(here[c], ni - 2, 1)
            total.append(
                2.0625 * here[c]
                + pltpu.roll(plus, ni - 1, 1)
                + pltpu.roll(minus, 1, 1)
                + wide * (1.0 / 32.0)
            )
        for direction, reader in ((2, rows), (3, layer)):
            above, below = reader(1), reader(-1)
            top, bottom = flux(above, direction), flux(below, direction)
            for c in range(5):
                total[c] = total[c] + 0.5 * (top[c] - bottom[c]) - 0.375 * (above[c] + below[c])
            above, below = reader(2), reader(-2)
            for c in range(5):
                total[c] = total[c] + (above[c] + below[c]) * (1.0 / 32.0)
        weight = -0.5 * blanking[pl.ds(k, cj, stride=ck), :].astype(F32)
        total = [t * weight for t in total]
        for c in range(5):
            right_side[c, pl.ds(k, cj, stride=ck), :] = total[c]
        mixed = mix(char_around, total)
        for c in range(5):
            first[c, k] = mixed[c]
        return carry

    def a_copy(dest):
        return pltpu.make_async_remote_copy(
            src_ref=asend.at[dest],
            dst_ref=x.at[:, :, pl.ds(pl.multiple_of(mj * cj, 8), cj), :],
            send_sem=a_send.at[dest],
            recv_sem=a_recv.at[mj],
            device_id={"ja": dest},
            device_id_type=MESH,
        )

    def around(start, count):
        out = []
        for c in range(5):
            high, low = halves(first[c, start : start + count].reshape(count * cj, ni))
            out.append(
                dot(jnp.concatenate([high, high, low], axis=1), around3[c], ((1,), (1,)))
            )
        out = mix(around_to_axial, out)
        for c in range(5):
            for s in range(count):
                k = start + s
                asend[k // kp, c, k % kp] = out[c][s * cj : (s + 1) * cj]
        for dest in range(start // kp, (start + count) // kp):

            @pl.when(dest != mj)
            def _():
                a_copy(dest).start()

    edge = 2
    lax.fori_loop(edge, ck - edge, plane, 0)
    around(edge, ck - 2 * edge)

    @pl.when(mk > 0)
    def _():
        khalo(True).wait_recv()

    @pl.when(mk < nka - 1)
    def _():
        khalo(False).wait_recv()

    lax.fori_loop(0, edge, plane, 0)
    around(0, edge)
    lax.fori_loop(ck - edge, ck, plane, 0)
    around(ck - edge, edge)

    own = pl.ds(pl.multiple_of(mj * cj, 8), cj)
    for c in range(5):
        for s in range(kp):
            x[c, s, own, :] = asend[mj, c, s]

    for o in range(1, nja):
        source = lax.rem(mj + o, nja)
        pltpu.make_async_remote_copy(
            src_ref=asend.at[source],
            dst_ref=x.at[:, :, pl.ds(pl.multiple_of(source * cj, 8), cj), :],
            send_sem=a_send.at[source],
            recv_sem=a_recv.at[source],
            device_id={"ja": source},
            device_id_type=MESH,
        ).wait_recv()

    for c in range(5):
        high, low = halves(jnp.concatenate([x[c, s] for s in range(kp)], axis=1))
        out = dot(axial3[c], jnp.concatenate([high, low, high], axis=0), ((1,), (0,)))
        for s in range(kp):
            solved[c, s] = out[:, s * ni : (s + 1) * ni]

    def b_copy(dest, source):
        return pltpu.make_async_remote_copy(
            src_ref=bsend.at[dest],
            dst_ref=y.at[:, pl.ds(pl.multiple_of(source * (kp * cj), 8), kp * cj), :],
            send_sem=b_send.at[dest],
            recv_sem=b_recv.at[source],
            device_id={"ja": dest},
            device_id_type=MESH,
        )

    for o in range(1, nja + 1):
        dest = lax.rem(mj + o, nja)
        for s in range(kp):
            block = [
                solved[c, s, pl.ds(pl.multiple_of(dest * cj, 8), cj), :] for c in range(5)
            ]
            block = mix(axial_to_normal, block)
            for c in range(5):
                if o < nja:
                    bsend[dest, c, s * cj : (s + 1) * cj, :] = block[c]
                else:
                    y[c, pl.ds(pl.multiple_of((mj * kp + s) * cj, 8), cj), :] = block[c]
        if o < nja:
            b_copy(dest, mj).start()
    for o in range(1, nja):
        source = lax.rem(mj + o, nja)
        b_copy(source, source).wait_recv()

    def w_copy(dest, source):
        return pltpu.make_async_remote_copy(
            src_ref=w.at[dest],
            dst_ref=z.at[:, :, pl.ds(pl.multiple_of(source * ck, 8), ck), :],
            send_sem=w_send.at[dest],
            recv_sem=w_recv.at[source],
            device_id={"ka": dest},
            device_id_type=MESH,
        )

    for o in range(1, nka + 1):
        dest = lax.rem(mk + o, nka)
        for s in range(jq):
            for c in range(5):
                tile = y[c, pl.ds(dest * jq + s, ck, stride=cj), :]
                if o < nka:
                    w[dest, c, s] = tile
                else:
                    z[c, s, pl.ds(pl.multiple_of(mk * ck, 8), ck), :] = tile
        if o < nka:
            w_copy(dest, mk).start()
    for o in range(1, nka):
        source = lax.rem(mk + o, nka)
        w_copy(source, source).wait_recv()

    for c in range(5):
        high, low = halves(jnp.concatenate([z[c, s] for s in range(jq)], axis=1))
        out = dot(normal3[c], jnp.concatenate([high, low, high], axis=0), ((1,), (0,)))
        for s in range(jq):
            normal[c, s] = out[:, s * ni : (s + 1) * ni]

    def c_copy(dest, source):
        return pltpu.make_async_remote_copy(
            src_ref=csend.at[dest],
            dst_ref=u.at[:, pl.ds(pl.multiple_of(source * (jq * ck), 8), jq * ck), :],
            send_sem=c_send.at[dest],
            recv_sem=c_recv.at[source],
            device_id={"ka": dest},
            device_id_type=MESH,
        )

    for o in range(1, nka + 1):
        dest = lax.rem(mk + o, nka)
        for s in range(jq):
            block = [
                normal[c, s, pl.ds(pl.multiple_of(dest * ck, 8), ck), :] for c in range(5)
            ]
            block = mix(char_back, block)
            for c in range(5):
                if o < nka:
                    csend[dest, c, s * ck : (s + 1) * ck, :] = block[c]
                else:
                    u[c, pl.ds(pl.multiple_of((mk * jq + s) * ck, 8), ck), :] = block[c]
        if o < nka:
            c_copy(dest, mk).start()
    for o in range(1, nka):
        source = lax.rem(mk + o, nka)
        c_copy(source, source).wait_recv()

    weight = blanking[...].astype(F32)
    for c in range(5):
        update[c] = u[c] * weight

    for upward, last, here in ((True, nja - 1, mj), (False, 0, mj)):

        @pl.when(here != last)
        def _(upward=upward):
            jhalo_copy(upward).wait_send()

    for upward, last, here in ((True, nka - 1, mk), (False, 0, mk)):

        @pl.when(here != last)
        def _(upward=upward):
            khalo(upward).wait_send()

    for o in range(1, nja):
        other = lax.rem(mj + o, nja)
        a_copy(other).wait_send()
        b_copy(other, mj).wait_send()
    for o in range(1, nka):
        other = lax.rem(mk + o, nka)
        w_copy(other, mk).wait_send()
        c_copy(other, mk).wait_send()


def body(
    conserved,
    blanking,
    wall_type,
    char_around,
    around_to_axial,
    axial_to_normal,
    char_back,
    around_inverse,
    axial_inverse,
    normal_inverse,
):
    nja = lax.axis_size("ja")
    nka = lax.axis_size("ka")
    _, cj, ck, ni = conserved.shape
    nj, nk = cj * nja, ck * nka
    kp, jq = ck // nja, cj // nka
    vmem = pl.BlockSpec(memory_space=pltpu.VMEM)
    flat = jax.ShapeDtypeStruct((5, cj * ck, ni), F32)
    dma = pltpu.SemaphoreType.DMA
    right_side, update = pl.pallas_call(
        functools.partial(kernel, nja, nka),
        out_shape=(flat, flat),
        in_specs=[pl.BlockSpec(memory_space=pltpu.HBM)] * 10,
        out_specs=(vmem, vmem),
        scratch_shapes=[
            pltpu.VMEM((5, cj * ck, ni), F32),
            pltpu.VMEM((cj * ck, ni), jnp.int32),
            pltpu.VMEM((cj, ni), jnp.int32),
            pltpu.SMEM((5, 5), F32),
            pltpu.SMEM((5, 5), F32),
            pltpu.SMEM((5, 5), F32),
            pltpu.SMEM((5, 5), F32),
            pltpu.VMEM((5, ni, ni), F32),
            pltpu.VMEM((5, nj, nj), F32),
            pltpu.VMEM((5, nk, nk), F32),
            pltpu.VMEM((5, ck + 4, cj + 16, ni), F32),
            pltpu.VMEM((2, 5, 2 * ck, ni), F32),
            pltpu.VMEM((5, ck, cj, ni), F32),
            pltpu.VMEM((nja, 5, kp, cj, ni), F32),
            pltpu.VMEM((5, kp, nj, ni), F32),
            pltpu.VMEM((5, kp, nj, ni), F32),
            pltpu.VMEM((nja, 5, kp * cj, ni), F32),
            pltpu.VMEM((5, ck * cj, ni), F32),
            pltpu.VMEM((nka, 5, jq, ck, ni), F32),
            pltpu.VMEM((5, jq, nk, ni), F32),
            pltpu.VMEM((5, jq, nk, ni), F32),
            pltpu.VMEM((nka, 5, jq * ck, ni), F32),
            pltpu.VMEM((5, cj * ck, ni), F32),
            pltpu.VMEM((5, ni, 3 * ni), BF16),
            pltpu.VMEM((5, nj, 3 * nj), BF16),
            pltpu.VMEM((5, nk, 3 * nk), BF16),
            dma((2, 2)),
            dma((2, 2)),
            dma((nja,)),
            dma((nja,)),
            dma((nja,)),
            dma((nja,)),
            dma((nka,)),
            dma((nka,)),
            dma((nka,)),
            dma((nka,)),
            dma((10,)),
        ],
        compiler_params=pltpu.CompilerParams(
            collective_id=0, has_side_effects=True, vmem_limit_bytes=64 * 1024 * 1024 - 65536
        ),
    )(
        conserved.reshape(5, cj * ck, ni),
        blanking.reshape(cj * ck, ni),
        wall_type,
        char_around,
        around_to_axial,
        axial_to_normal,
        char_back,
        around_inverse,
        axial_inverse,
        normal_inverse,
    )
    return right_side.reshape(conserved.shape), update.reshape(conserved.shape)


def solution(mesh):
    slabs = P(None, "ja", "ka", None)
    return jax.shard_map(
        body,
        mesh=mesh,
        in_specs=(slabs, P("ja", "ka", None), P("ja", None)) + (P(),) * 7,
        out_specs=(slabs, slabs),
        check_vma=False,
    )
```

```python
import functools

import jax
import jax.numpy as jnp
from jax import lax
from jax.experimental import pallas as pl
from jax.experimental.pallas import tpu as pltpu
from jax.sharding import PartitionSpec as P

F32 = jnp.float32
BF16 = jnp.bfloat16
MESH = pl.DeviceIdType.MESH
FREESTREAM = (1.0, 0.4, 0.1, 0.0, 2.585)
TOP = 8


def flux(state, direction):
    inverse = 1.0 / state[0]
    kinetic = state[1] * state[1] + state[2] * state[2] + state[3] * state[3]
    pressure = 0.4 * (state[4] - 0.5 * kinetic * inverse)
    velocity = state[direction] * inverse
    pieces = [state[direction]]
    for member in (1, 2, 3):
        piece = state[member] * velocity
        pieces.append(piece + pressure if member == direction else piece)
    pieces.append((state[4] + pressure) * velocity)
    return pieces


def mix(matrix, values):
    out = []
    for a in range(5):
        total = matrix[a, 0] * values[0]
        for b in range(1, 5):
            total = total + matrix[a, b] * values[b]
        out.append(total)
    return out


def halves(x):
    high = x.astype(BF16)
    return high, (x - high.astype(F32)).astype(BF16)


def dot(x, y, dims):
    return lax.dot_general(x, y, (dims, ((), ())), preferred_element_type=F32)


def kernel(
    nja,
    nka,
    *refs,
):
    sources, refs = refs[:10], refs[10:]
    right_side, update = refs[:2]
    inputs, refs = refs[2:12], refs[12:]
    (
        cells,
        blanking,
        wall,
        char_around,
        around_to_axial,
        axial_to_normal,
        char_back,
        around_inverse,
        axial_inverse,
        normal_inverse,
    ) = inputs
    (
        q,
        jhalo,
        first,
        asend,
        x,
        solved,
        bsend,
        y,
        w,
        z,
        normal,
        csend,
        u,
        around3,
        axial3,
        normal3,
        jsem,
        ksem,
        a_send,
        a_recv,
        b_send,
        b_recv,
        w_send,
        w_recv,
        c_send,
        c_recv,
        insem,
    ) = refs
    loads = [
        pltpu.make_async_copy(source, held, insem.at[n])
        for n, (source, held) in enumerate(zip(sources, inputs))
    ]
    for load in loads:
        load.start()
    cj = wall.shape[0]
    ck = cells.shape[1] // cj
    ni = cells.shape[2]
    kp = ck // nja
    jq = cj // nka
    mj = lax.axis_index("ja")
    mk = lax.axis_index("ka")

    barrier = pltpu.get_barrier_semaphore()
    for o in range(1, nja):
        pl.semaphore_signal(
            barrier, inc=1, device_id={"ja": lax.rem(mj + o, nja)}, device_id_type=MESH
        )
    for o in range(1, nka):
        pl.semaphore_signal(
            barrier, inc=1, device_id={"ka": lax.rem(mk + o, nka)}, device_id_type=MESH
        )

    loads[0].wait()

    def spread(k, carry):
        for c in range(5):
            q[c, k + 2, TOP : TOP + cj, :] = cells[c, pl.ds(k, cj, stride=ck), :]
        return carry

    lax.fori_loop(0, ck, spread, 0)
    pl.semaphore_wait(barrier, nja - 1 + nka - 1)

    def khalo(upward):
        if upward:
            src, dst, other = ck, 0, mk + 1
        else:
            src, dst, other = 2, ck + 2, mk - 1
        return pltpu.make_async_remote_copy(
            src_ref=q.at[:, src : src + 2, TOP : TOP + cj, :],
            dst_ref=q.at[:, dst : dst + 2, TOP : TOP + cj, :],
            send_sem=ksem.at[0, int(upward)],
            recv_sem=ksem.at[1, int(upward)],
            device_id={"ka": other},
            device_id_type=MESH,
        )

    def jhalo_copy(upward):
        if upward:
            src, dst, other = (cj - 2) * ck, 0, mj + 1
        else:
            src, dst, other = 0, 1, mj - 1
        return pltpu.make_async_remote_copy(
            src_ref=cells.at[:, src : src + 2 * ck, :],
            dst_ref=jhalo.at[dst],
            send_sem=jsem.at[0, int(upward)],
            recv_sem=jsem.at[1, int(upward)],
            device_id={"ja": other},
            device_id_type=MESH,
        )

    @pl.when(mj < nja - 1)
    def _():
        jhalo_copy(True).start()

    @pl.when(mj > 0)
    def _():
        jhalo_copy(False).start()

    @pl.when(mk < nka - 1)
    def _():
        khalo(True).start()

    @pl.when(mk > 0)
    def _():
        khalo(False).start()

    for load in loads[1:]:
        load.wait()

    @pl.when(mj == 0)
    def _():
        for c in range(5):
            jhalo[0, c] = jnp.full((2 * ck, ni), FREESTREAM[c], F32)

    @pl.when(mj == nja - 1)
    def _():
        for c in range(5):
            jhalo[1, c] = jnp.full((2 * ck, ni), FREESTREAM[c], F32)

    @pl.when(mk == 0)
    def _():
        kind = wall[...]
        for c in range(5):
            near = q[c, 2, TOP : TOP + cj, :]
            far = q[c, 3, TOP : TOP + cj, :]
            sign = -1.0 if c == 3 else 1.0
            rest = jnp.where(kind == 1, near, FREESTREAM[c])
            q[c, 1, TOP : TOP + cj, :] = jnp.where(kind == 0, sign * near, rest)
            q[c, 0, TOP : TOP + cj, :] = jnp.where(kind == 0, sign * far, rest)

    @pl.when(mk == nka - 1)
    def _():
        for c in range(5):
            for r in range(2):
                q[c, ck + 2 + r, TOP : TOP + cj, :] = jnp.full((cj, ni), FREESTREAM[c], F32)

    for c in range(5):
        high, low = halves(around_inverse[c])
        around3[c] = jnp.concatenate([high, low, high], axis=1)
        rows = [
            axial_inverse[c, pl.ds(p * cj + s, nka, stride=jq), :]
            for p in range(nja)
            for s in range(jq)
        ]
        high, low = halves(jnp.concatenate(rows, axis=0))
        axial3[c] = jnp.concatenate([high, high, low], axis=1)
        high, low = halves(normal_inverse[c])
        normal3[c] = jnp.concatenate([high, high, low], axis=1)

    @pl.when(mj > 0)
    def _():
        jhalo_copy(True).wait_recv()

    @pl.when(mj < nja - 1)
    def _():
        jhalo_copy(False).wait_recv()

    def plane(k, carry):
        at = k + 2
        for c in range(5):
            for r in range(2):
                row = pl.ds(r * ck + k, 1)
                q[c, at, TOP - 2 + r : TOP - 1 + r, :] = jhalo[0, c, row, :]
                q[c, at, TOP + cj + r : TOP + cj + r + 1, :] = jhalo[1, c, row, :]

        def rows(offset):
            return [q[c, at, TOP + offset : TOP + offset + cj, :] for c in range(5)]

        def layer(offset):
            return [q[c, at + offset, TOP : TOP + cj, :] for c in range(5)]

        here = rows(0)
        flow = flux(here, 1)
        total = []
        for c in range(5):
            plus = 0.5 * flow[c] - 0.375 * here[c]
            minus = -0.5 * flow[c] - 0.375 * here[c]
            wide = pltpu.roll(here[c], 2, 1) + pltpu.roll(here[c], ni - 2, 1)
            total.append(
                2.0625 * here[c]
                + pltpu.roll(plus, ni - 1, 1)
                + pltpu.roll(minus, 1, 1)
                + wide * (1.0 / 32.0)
            )
        for direction, reader in ((2, rows), (3, layer)):
            above, below = reader(1), reader(-1)
            top, bottom = flux(above, direction), flux(below, direction)
            for c in range(5):
                total[c] = total[c] + 0.5 * (top[c] - bottom[c]) - 0.375 * (above[c] + below[c])
            above, below = reader(2), reader(-2)
            for c in range(5):
                total[c] = total[c] + (above[c] + below[c]) * (1.0 / 32.0)
        weight = -0.5 * blanking[pl.ds(k, cj, stride=ck), :].astype(F32)
        total = [t * weight for t in total]
        for c in range(5):
            right_side[c, pl.ds(k, cj, stride=ck), :] = total[c]
        mixed = mix(char_around, total)
        for c in range(5):
            first[c, k] = mixed[c]
        return carry

    def a_copy(dest):
        return pltpu.make_async_remote_copy(
            src_ref=asend.at[dest],
            dst_ref=x.at[:, :, pl.ds(pl.multiple_of(mj * cj, 8), cj), :],
            send_sem=a_send.at[dest],
            recv_sem=a_recv.at[mj],
            device_id={"ja": dest},
            device_id_type=MESH,
        )

    def around(start, count):
        out = []
        for c in range(5):
            high, low = halves(first[c, start : start + count].reshape(count * cj, ni))
            out.append(
                dot(jnp.concatenate([high, high, low], axis=1), around3[c], ((1,), (1,)))
            )
        out = mix(around_to_axial, out)
        for c in range(5):
            for s in range(count):
                k = start + s
                asend[k // kp, c, k % kp] = out[c][s * cj : (s + 1) * cj]
        for dest in range(start // kp, (start + count) // kp):

            @pl.when(dest != mj)
            def _():
                a_copy(dest).start()

    edge = 2
    lax.fori_loop(edge, ck - edge, plane, 0)
    around(edge, ck - 2 * edge)

    @pl.when(mk > 0)
    def _():
        khalo(True).wait_recv()

    @pl.when(mk < nka - 1)
    def _():
        khalo(False).wait_recv()

    lax.fori_loop(0, edge, plane, 0)
    around(0, edge)
    lax.fori_loop(ck - edge, ck, plane, 0)
    around(ck - edge, edge)

    own = pl.ds(pl.multiple_of(mj * cj, 8), cj)
    for c in range(5):
        for s in range(kp):
            x[c, s, own, :] = asend[mj, c, s]

    for o in range(1, nja):
        source = lax.rem(mj + o, nja)
        pltpu.make_async_remote_copy(
            src_ref=asend.at[source],
            dst_ref=x.at[:, :, pl.ds(pl.multiple_of(source * cj, 8), cj), :],
            send_sem=a_send.at[source],
            recv_sem=a_recv.at[source],
            device_id={"ja": source},
            device_id_type=MESH,
        ).wait_recv()

    for c in range(5):
        high, low = halves(jnp.concatenate([x[c, s] for s in range(kp)], axis=1))
        out = dot(axial3[c], jnp.concatenate([high, low, high], axis=0), ((1,), (0,)))
        for s in range(kp):
            solved[c, s] = out[:, s * ni : (s + 1) * ni]

    def b_copy(dest, source, s):
        return pltpu.make_async_remote_copy(
            src_ref=bsend.at[dest, s],
            dst_ref=y.at[s, :, pl.ds(pl.multiple_of(source * (kp * nka), 8), kp * nka), :],
            send_sem=b_send.at[dest, s],
            recv_sem=b_recv.at[source, s],
            device_id={"ja": dest},
            device_id_type=MESH,
        )

    for s in range(jq):
        for o in range(1, nja + 1):
            dest = lax.rem(mj + o, nja)
            for t in range(kp):
                rows = pl.ds(pl.multiple_of(dest * cj + s * nka, 8), nka)
                block = mix(axial_to_normal, [solved[c, t, rows, :] for c in range(5)])
                for c in range(5):
                    if o < nja:
                        bsend[dest, s, c, t * nka : (t + 1) * nka, :] = block[c]
                    else:
                        rows = pl.ds(pl.multiple_of((mj * kp + t) * nka, 8), nka)
                        y[s, c, rows, :] = block[c]
            if o < nja:
                b_copy(dest, mj, s).start()

    def w_copy(dest, source, s):
        return pltpu.make_async_remote_copy(
            src_ref=w.at[dest, s],
            dst_ref=z.at[s, :, pl.ds(pl.multiple_of(source * ck, 8), ck), :],
            send_sem=w_send.at[dest, s],
            recv_sem=w_recv.at[source, s],
            device_id={"ka": dest},
            device_id_type=MESH,
        )

    for s in range(jq):
        for o in range(1, nja):
            source = lax.rem(mj + o, nja)
            b_copy(source, source, s).wait_recv()
        for o in range(1, nka + 1):
            dest = lax.rem(mk + o, nka)
            for c in range(5):
                tile = y[s, c, pl.ds(dest, ck, stride=nka), :]
                if o < nka:
                    w[dest, s, c] = tile
                else:
                    z[s, c, pl.ds(pl.multiple_of(mk * ck, 8), ck), :] = tile
            if o < nka:
                w_copy(dest, mk, s).start()

    def c_copy(dest, source, s):
        return pltpu.make_async_remote_copy(
            src_ref=csend.at[dest, s],
            dst_ref=u.at[:, pl.ds(pl.multiple_of((source * jq + s) * ck, 8), ck), :],
            send_sem=c_send.at[dest, s],
            recv_sem=c_recv.at[source, s],
            device_id={"ka": dest},
            device_id_type=MESH,
        )

    for s in range(jq):
        for o in range(1, nka):
            source = lax.rem(mk + o, nka)
            w_copy(source, source, s).wait_recv()
        for c in range(5):
            high, low = halves(z[s, c])
            normal[s, c] = dot(
                normal3[c], jnp.concatenate([high, low, high], axis=0), ((1,), (0,))
            )
        for o in range(1, nka + 1):
            dest = lax.rem(mk + o, nka)
            rows = pl.ds(pl.multiple_of(dest * ck, 8), ck)
            block = mix(char_back, [normal[s, c, rows, :] for c in range(5)])
            for c in range(5):
                if o < nka:
                    csend[dest, s, c] = block[c]
                else:
                    u[c, pl.ds(pl.multiple_of((mk * jq + s) * ck, 8), ck), :] = block[c]
            if o < nka:
                c_copy(dest, mk, s).start()
    for s in range(jq):
        for o in range(1, nka):
            source = lax.rem(mk + o, nka)
            c_copy(source, source, s).wait_recv()

    weight = blanking[...].astype(F32)
    for c in range(5):
        update[c] = u[c] * weight

    for upward, last, here in ((True, nja - 1, mj), (False, 0, mj)):

        @pl.when(here != last)
        def _(upward=upward):
            jhalo_copy(upward).wait_send()

    for upward, last, here in ((True, nka - 1, mk), (False, 0, mk)):

        @pl.when(here != last)
        def _(upward=upward):
            khalo(upward).wait_send()

    for o in range(1, nja):
        other = lax.rem(mj + o, nja)
        a_copy(other).wait_send()
        for s in range(jq):
            b_copy(other, mj, s).wait_send()
    for o in range(1, nka):
        other = lax.rem(mk + o, nka)
        for s in range(jq):
            w_copy(other, mk, s).wait_send()
            c_copy(other, mk, s).wait_send()


def body(
    conserved,
    blanking,
    wall_type,
    char_around,
    around_to_axial,
    axial_to_normal,
    char_back,
    around_inverse,
    axial_inverse,
    normal_inverse,
):
    nja = lax.axis_size("ja")
    nka = lax.axis_size("ka")
    _, cj, ck, ni = conserved.shape
    nj, nk = cj * nja, ck * nka
    kp, jq = ck // nja, cj // nka
    vmem = pl.BlockSpec(memory_space=pltpu.VMEM)
    flat = jax.ShapeDtypeStruct((5, cj * ck, ni), F32)
    dma = pltpu.SemaphoreType.DMA
    right_side, update = pl.pallas_call(
        functools.partial(kernel, nja, nka),
        out_shape=(flat, flat),
        in_specs=[pl.BlockSpec(memory_space=pltpu.HBM)] * 10,
        out_specs=(vmem, vmem),
        scratch_shapes=[
            pltpu.VMEM((5, cj * ck, ni), F32),
            pltpu.VMEM((cj * ck, ni), jnp.int32),
            pltpu.VMEM((cj, ni), jnp.int32),
            pltpu.SMEM((5, 5), F32),
            pltpu.SMEM((5, 5), F32),
            pltpu.SMEM((5, 5), F32),
            pltpu.SMEM((5, 5), F32),
            pltpu.VMEM((5, ni, ni), F32),
            pltpu.VMEM((5, nj, nj), F32),
            pltpu.VMEM((5, nk, nk), F32),
            pltpu.VMEM((5, ck + 4, cj + 16, ni), F32),
            pltpu.VMEM((2, 5, 2 * ck, ni), F32),
            pltpu.VMEM((5, ck, cj, ni), F32),
            pltpu.VMEM((nja, 5, kp, cj, ni), F32),
            pltpu.VMEM((5, kp, nj, ni), F32),
            pltpu.VMEM((5, kp, nj, ni), F32),
            pltpu.VMEM((nja, jq, 5, kp * nka, ni), F32),
            pltpu.VMEM((jq, 5, ck * nka, ni), F32),
            pltpu.VMEM((nka, jq, 5, ck, ni), F32),
            pltpu.VMEM((jq, 5, nk, ni), F32),
            pltpu.VMEM((jq, 5, nk, ni), F32),
            pltpu.VMEM((nka, jq, 5, ck, ni), F32),
            pltpu.VMEM((5, cj * ck, ni), F32),
            pltpu.VMEM((5, ni, 3 * ni), BF16),
            pltpu.VMEM((5, nj, 3 * nj), BF16),
            pltpu.VMEM((5, nk, 3 * nk), BF16),
            dma((2, 2)),
            dma((2, 2)),
            dma((nja,)),
            dma((nja,)),
            dma((nja, jq)),
            dma((nja, jq)),
            dma((nka, jq)),
            dma((nka, jq)),
            dma((nka, jq)),
            dma((nka, jq)),
            dma((10,)),
        ],
        compiler_params=pltpu.CompilerParams(
            collective_id=0, has_side_effects=True, vmem_limit_bytes=64 * 1024 * 1024 - 65536
        ),
    )(
        conserved.reshape(5, cj * ck, ni),
        blanking.reshape(cj * ck, ni),
        wall_type,
        char_around,
        around_to_axial,
        axial_to_normal,
        char_back,
        around_inverse,
        axial_inverse,
        normal_inverse,
    )
    return right_side.reshape(conserved.shape), update.reshape(conserved.shape)


def solution(mesh):
    slabs = P(None, "ja", "ka", None)
    return jax.shard_map(
        body,
        mesh=mesh,
        in_specs=(slabs, P("ja", "ka", None), P("ja", None)) + (P(),) * 7,
        out_specs=(slabs, slabs),
        check_vma=False,
    )
```

```python
import functools

import jax
import jax.numpy as jnp
from jax import lax
from jax.experimental import pallas as pl
from jax.experimental.pallas import tpu as pltpu
from jax.sharding import PartitionSpec as P

F32 = jnp.float32
BF16 = jnp.bfloat16
MESH = pl.DeviceIdType.MESH
FREESTREAM = (1.0, 0.4, 0.1, 0.0, 2.585)
TOP = 8


def flux(state, direction):
    inverse = 1.0 / state[0]
    kinetic = state[1] * state[1] + state[2] * state[2] + state[3] * state[3]
    pressure = 0.4 * (state[4] - 0.5 * kinetic * inverse)
    velocity = state[direction] * inverse
    pieces = [state[direction]]
    for member in (1, 2, 3):
        piece = state[member] * velocity
        pieces.append(piece + pressure if member == direction else piece)
    pieces.append((state[4] + pressure) * velocity)
    return pieces


def mix(matrix, values):
    out = []
    for a in range(5):
        total = matrix[a, 0] * values[0]
        for b in range(1, 5):
            total = total + matrix[a, b] * values[b]
        out.append(total)
    return out


def halves(x):
    high = x.astype(BF16)
    return high, (x - high.astype(F32)).astype(BF16)


def dot(x, y, dims):
    return lax.dot_general(x, y, (dims, ((), ())), preferred_element_type=F32)


def kernel(
    nja,
    nka,
    *refs,
):
    sources, refs = refs[:10], refs[10:]
    right_side, update, active = refs[:3]
    inputs, refs = refs[3:13], refs[13:]
    (
        cells,
        blanking,
        wall,
        char_around,
        around_to_axial,
        axial_to_normal,
        char_back,
        around_inverse,
        axial_inverse,
        normal_inverse,
    ) = inputs
    (
        q,
        jhalo,
        first,
        asend,
        x,
        solved,
        bsend,
        y,
        w,
        z,
        normal,
        csend,
        u,
        around3,
        axial3,
        normal3,
        jsem,
        ksem,
        a_send,
        a_recv,
        b_send,
        b_recv,
        w_send,
        w_recv,
        c_send,
        c_recv,
        insem,
    ) = refs
    loads = [
        pltpu.make_async_copy(source, held, insem.at[n])
        for n, (source, held) in enumerate(zip(sources, inputs))
    ]
    for load in loads:
        load.start()
    cj = wall.shape[0]
    ck = cells.shape[1] // cj
    ni = cells.shape[2]
    kp = ck // nja
    jq = cj // nka
    mj = lax.axis_index("ja")
    mk = lax.axis_index("ka")

    barrier = pltpu.get_barrier_semaphore()
    for o in range(1, nja):
        pl.semaphore_signal(
            barrier, inc=1, device_id={"ja": lax.rem(mj + o, nja)}, device_id_type=MESH
        )
    for o in range(1, nka):
        pl.semaphore_signal(
            barrier, inc=1, device_id={"ka": lax.rem(mk + o, nka)}, device_id_type=MESH
        )

    loads[0].wait()

    def spread(k, carry):
        for c in range(5):
            q[c, k + 2, TOP : TOP + cj, :] = cells[c, pl.ds(k, cj, stride=ck), :]
        return carry

    lax.fori_loop(0, ck, spread, 0)
    pl.semaphore_wait(barrier, nja - 1 + nka - 1)

    def khalo(upward):
        if upward:
            src, dst, other = ck, 0, mk + 1
        else:
            src, dst, other = 2, ck + 2, mk - 1
        return pltpu.make_async_remote_copy(
            src_ref=q.at[:, src : src + 2, TOP : TOP + cj, :],
            dst_ref=q.at[:, dst : dst + 2, TOP : TOP + cj, :],
            send_sem=ksem.at[0, int(upward)],
            recv_sem=ksem.at[1, int(upward)],
            device_id={"ka": other},
            device_id_type=MESH,
        )

    def jhalo_copy(upward):
        if upward:
            src, dst, other = (cj - 2) * ck, 0, mj + 1
        else:
            src, dst, other = 0, 1, mj - 1
        return pltpu.make_async_remote_copy(
            src_ref=cells.at[:, src : src + 2 * ck, :],
            dst_ref=jhalo.at[dst],
            send_sem=jsem.at[0, int(upward)],
            recv_sem=jsem.at[1, int(upward)],
            device_id={"ja": other},
            device_id_type=MESH,
        )

    @pl.when(mj < nja - 1)
    def _():
        jhalo_copy(True).start()

    @pl.when(mj > 0)
    def _():
        jhalo_copy(False).start()

    @pl.when(mk < nka - 1)
    def _():
        khalo(True).start()

    @pl.when(mk > 0)
    def _():
        khalo(False).start()

    for load in loads[1:]:
        load.wait()

    @pl.when(mj == 0)
    def _():
        for c in range(5):
            jhalo[0, c] = jnp.full((2 * ck, ni), FREESTREAM[c], F32)

    @pl.when(mj == nja - 1)
    def _():
        for c in range(5):
            jhalo[1, c] = jnp.full((2 * ck, ni), FREESTREAM[c], F32)

    @pl.when(mk == 0)
    def _():
        kind = wall[...]
        for c in range(5):
            near = q[c, 2, TOP : TOP + cj, :]
            far = q[c, 3, TOP : TOP + cj, :]
            sign = -1.0 if c == 3 else 1.0
            rest = jnp.where(kind == 1, near, FREESTREAM[c])
            q[c, 1, TOP : TOP + cj, :] = jnp.where(kind == 0, sign * near, rest)
            q[c, 0, TOP : TOP + cj, :] = jnp.where(kind == 0, sign * far, rest)

    @pl.when(mk == nka - 1)
    def _():
        for c in range(5):
            for r in range(2):
                q[c, ck + 2 + r, TOP : TOP + cj, :] = jnp.full((cj, ni), FREESTREAM[c], F32)

    for c in range(5):
        high, low = halves(around_inverse[c])
        around3[c] = jnp.concatenate([high, low, high], axis=1)
        rows = [
            axial_inverse[c, pl.ds(p * cj + s, nka, stride=jq), :]
            for p in range(nja)
            for s in range(jq)
        ]
        high, low = halves(jnp.concatenate(rows, axis=0))
        axial3[c] = jnp.concatenate([high, high, low], axis=1)
        high, low = halves(normal_inverse[c])
        normal3[c] = jnp.concatenate([high, high, low], axis=1)

    @pl.when(mj > 0)
    def _():
        jhalo_copy(True).wait_recv()

    @pl.when(mj < nja - 1)
    def _():
        jhalo_copy(False).wait_recv()

    def plane(k, carry):
        at = k + 2
        for c in range(5):
            for r in range(2):
                row = pl.ds(r * ck + k, 1)
                q[c, at, TOP - 2 + r : TOP - 1 + r, :] = jhalo[0, c, row, :]
                q[c, at, TOP + cj + r : TOP + cj + r + 1, :] = jhalo[1, c, row, :]

        def rows(offset):
            return [q[c, at, TOP + offset : TOP + offset + cj, :] for c in range(5)]

        def layer(offset):
            return [q[c, at + offset, TOP : TOP + cj, :] for c in range(5)]

        here = rows(0)
        flow = flux(here, 1)
        total = []
        for c in range(5):
            plus = 0.5 * flow[c] - 0.375 * here[c]
            minus = -0.5 * flow[c] - 0.375 * here[c]
            wide = pltpu.roll(here[c], 2, 1) + pltpu.roll(here[c], ni - 2, 1)
            total.append(
                2.0625 * here[c]
                + pltpu.roll(plus, ni - 1, 1)
                + pltpu.roll(minus, 1, 1)
                + wide * (1.0 / 32.0)
            )
        for direction, reader in ((2, rows), (3, layer)):
            above, below = reader(1), reader(-1)
            top, bottom = flux(above, direction), flux(below, direction)
            for c in range(5):
                total[c] = total[c] + 0.5 * (top[c] - bottom[c]) - 0.375 * (above[c] + below[c])
            above, below = reader(2), reader(-2)
            for c in range(5):
                total[c] = total[c] + (above[c] + below[c]) * (1.0 / 32.0)
        weight = blanking[pl.ds(k, cj, stride=ck), :].astype(F32)
        total = [t * weight for t in total]
        for c in range(5):
            right_side[c, pl.ds(k, cj, stride=ck), :] = total[c]
        mixed = mix(char_around, [-0.5 * t for t in total])
        for c in range(5):
            first[c, k] = mixed[c]
        return carry

    def a_copy(dest):
        return pltpu.make_async_remote_copy(
            src_ref=asend.at[dest],
            dst_ref=x.at[:, :, pl.ds(pl.multiple_of(mj * cj, 8), cj), :],
            send_sem=a_send.at[dest],
            recv_sem=a_recv.at[mj],
            device_id={"ja": dest},
            device_id_type=MESH,
        )

    def around(start, count):
        out = []
        for c in range(5):
            high, low = halves(first[c, start : start + count].reshape(count * cj, ni))
            out.append(
                dot(jnp.concatenate([high, high, low], axis=1), around3[c], ((1,), (1,)))
            )
        out = mix(around_to_axial, out)
        for c in range(5):
            for s in range(count):
                k = start + s
                asend[k // kp, c, k % kp] = out[c][s * cj : (s + 1) * cj]
        for dest in range(start // kp, (start + count) // kp):

            @pl.when(dest != mj)
            def _():
                a_copy(dest).start()

    edge = 2
    lax.fori_loop(edge, ck - edge, plane, 0)
    around(edge, ck - 2 * edge)

    @pl.when(mk > 0)
    def _():
        khalo(True).wait_recv()

    @pl.when(mk < nka - 1)
    def _():
        khalo(False).wait_recv()

    lax.fori_loop(0, edge, plane, 0)
    around(0, edge)
    lax.fori_loop(ck - edge, ck, plane, 0)
    around(ck - edge, edge)

    own = pl.ds(pl.multiple_of(mj * cj, 8), cj)
    for c in range(5):
        for s in range(kp):
            x[c, s, own, :] = asend[mj, c, s]

    for o in range(1, nja):
        source = lax.rem(mj + o, nja)
        pltpu.make_async_remote_copy(
            src_ref=asend.at[source],
            dst_ref=x.at[:, :, pl.ds(pl.multiple_of(source * cj, 8), cj), :],
            send_sem=a_send.at[source],
            recv_sem=a_recv.at[source],
            device_id={"ja": source},
            device_id_type=MESH,
        ).wait_recv()

    for c in range(5):
        high, low = halves(jnp.concatenate([x[c, s] for s in range(kp)], axis=1))
        out = dot(axial3[c], jnp.concatenate([high, low, high], axis=0), ((1,), (0,)))
        for s in range(kp):
            solved[c, s] = out[:, s * ni : (s + 1) * ni]

    def b_copy(dest, source, s):
        return pltpu.make_async_remote_copy(
            src_ref=bsend.at[dest, s],
            dst_ref=y.at[s, :, pl.ds(pl.multiple_of(source * (kp * nka), 8), kp * nka), :],
            send_sem=b_send.at[dest, s],
            recv_sem=b_recv.at[source, s],
            device_id={"ja": dest},
            device_id_type=MESH,
        )

    for s in range(jq):
        for o in range(1, nja + 1):
            dest = lax.rem(mj + o, nja)
            for t in range(kp):
                rows = pl.ds(pl.multiple_of(dest * cj + s * nka, 8), nka)
                block = mix(axial_to_normal, [solved[c, t, rows, :] for c in range(5)])
                for c in range(5):
                    if o < nja:
                        bsend[dest, s, c, t * nka : (t + 1) * nka, :] = block[c]
                    else:
                        rows = pl.ds(pl.multiple_of((mj * kp + t) * nka, 8), nka)
                        y[s, c, rows, :] = block[c]
            if o < nja:
                b_copy(dest, mj, s).start()

    def w_copy(dest, source, s):
        return pltpu.make_async_remote_copy(
            src_ref=w.at[dest, s],
            dst_ref=z.at[s, :, pl.ds(pl.multiple_of(source * ck, 8), ck), :],
            send_sem=w_send.at[dest, s],
            recv_sem=w_recv.at[source, s],
            device_id={"ka": dest},
            device_id_type=MESH,
        )

    for s in range(jq):
        for o in range(1, nja):
            source = lax.rem(mj + o, nja)
            b_copy(source, source, s).wait_recv()
        for o in range(1, nka + 1):
            dest = lax.rem(mk + o, nka)
            for c in range(5):
                tile = y[s, c, pl.ds(dest, ck, stride=nka), :]
                if o < nka:
                    w[dest, s, c] = tile
                else:
                    z[s, c, pl.ds(pl.multiple_of(mk * ck, 8), ck), :] = tile
            if o < nka:
                w_copy(dest, mk, s).start()

    def c_copy(dest, source, s):
        return pltpu.make_async_remote_copy(
            src_ref=csend.at[dest, s],
            dst_ref=u.at[:, pl.ds(pl.multiple_of((source * jq + s) * ck, 8), ck), :],
            send_sem=c_send.at[dest, s],
            recv_sem=c_recv.at[source, s],
            device_id={"ka": dest},
            device_id_type=MESH,
        )

    for s in range(jq):
        for o in range(1, nka):
            source = lax.rem(mk + o, nka)
            w_copy(source, source, s).wait_recv()
        for c in range(5):
            high, low = halves(z[s, c])
            normal[s, c] = dot(
                normal3[c], jnp.concatenate([high, low, high], axis=0), ((1,), (0,))
            )
        for o in range(1, nka + 1):
            dest = lax.rem(mk + o, nka)
            rows = pl.ds(pl.multiple_of(dest * ck, 8), ck)
            block = mix(char_back, [normal[s, c, rows, :] for c in range(5)])
            for c in range(5):
                if o < nka:
                    csend[dest, s, c] = block[c]
                else:
                    u[c, pl.ds(pl.multiple_of((mk * jq + s) * ck, 8), ck), :] = block[c]
            if o < nka:
                c_copy(dest, mk, s).start()
    for s in range(jq):
        for o in range(1, nka):
            source = lax.rem(mk + o, nka)
            c_copy(source, source, s).wait_recv()

    active[...] = blanking[...].astype(F32)
    for c in range(5):
        update[c] = u[c]

    for upward, last, here in ((True, nja - 1, mj), (False, 0, mj)):

        @pl.when(here != last)
        def _(upward=upward):
            jhalo_copy(upward).wait_send()

    for upward, last, here in ((True, nka - 1, mk), (False, 0, mk)):

        @pl.when(here != last)
        def _(upward=upward):
            khalo(upward).wait_send()

    for o in range(1, nja):
        other = lax.rem(mj + o, nja)
        a_copy(other).wait_send()
        for s in range(jq):
            b_copy(other, mj, s).wait_send()
    for o in range(1, nka):
        other = lax.rem(mk + o, nka)
        for s in range(jq):
            w_copy(other, mk, s).wait_send()
            c_copy(other, mk, s).wait_send()


def body(
    conserved,
    blanking,
    wall_type,
    char_around,
    around_to_axial,
    axial_to_normal,
    char_back,
    around_inverse,
    axial_inverse,
    normal_inverse,
):
    nja = lax.axis_size("ja")
    nka = lax.axis_size("ka")
    _, cj, ck, ni = conserved.shape
    nj, nk = cj * nja, ck * nka
    kp, jq = ck // nja, cj // nka
    vmem = pl.BlockSpec(memory_space=pltpu.VMEM)
    flat = jax.ShapeDtypeStruct((5, cj * ck, ni), F32)
    dma = pltpu.SemaphoreType.DMA
    right_side, update, active = pl.pallas_call(
        functools.partial(kernel, nja, nka),
        out_shape=(flat, flat, jax.ShapeDtypeStruct((cj * ck, ni), F32)),
        in_specs=[pl.BlockSpec(memory_space=pltpu.HBM)] * 10,
        out_specs=(vmem, vmem, vmem),
        scratch_shapes=[
            pltpu.VMEM((5, cj * ck, ni), F32),
            pltpu.VMEM((cj * ck, ni), jnp.int32),
            pltpu.VMEM((cj, ni), jnp.int32),
            pltpu.SMEM((5, 5), F32),
            pltpu.SMEM((5, 5), F32),
            pltpu.SMEM((5, 5), F32),
            pltpu.SMEM((5, 5), F32),
            pltpu.VMEM((5, ni, ni), F32),
            pltpu.VMEM((5, nj, nj), F32),
            pltpu.VMEM((5, nk, nk), F32),
            pltpu.VMEM((5, ck + 4, cj + 16, ni), F32),
            pltpu.VMEM((2, 5, 2 * ck, ni), F32),
            pltpu.VMEM((5, ck, cj, ni), F32),
            pltpu.VMEM((nja, 5, kp, cj, ni), F32),
            pltpu.VMEM((5, kp, nj, ni), F32),
            pltpu.VMEM((5, kp, nj, ni), F32),
            pltpu.VMEM((nja, jq, 5, kp * nka, ni), F32),
            pltpu.VMEM((jq, 5, ck * nka, ni), F32),
            pltpu.VMEM((nka, jq, 5, ck, ni), F32),
            pltpu.VMEM((jq, 5, nk, ni), F32),
            pltpu.VMEM((jq, 5, nk, ni), F32),
            pltpu.VMEM((nka, jq, 5, ck, ni), F32),
            pltpu.VMEM((5, cj * ck, ni), F32),
            pltpu.VMEM((5, ni, 3 * ni), BF16),
            pltpu.VMEM((5, nj, 3 * nj), BF16),
            pltpu.VMEM((5, nk, 3 * nk), BF16),
            dma((2, 2)),
            dma((2, 2)),
            dma((nja,)),
            dma((nja,)),
            dma((nja, jq)),
            dma((nja, jq)),
            dma((nka, jq)),
            dma((nka, jq)),
            dma((nka, jq)),
            dma((nka, jq)),
            dma((10,)),
        ],
        compiler_params=pltpu.CompilerParams(
            collective_id=0, has_side_effects=True, vmem_limit_bytes=64 * 1024 * 1024 - 65536
        ),
    )(
        conserved.reshape(5, cj * ck, ni),
        blanking.reshape(cj * ck, ni),
        wall_type,
        char_around,
        around_to_axial,
        axial_to_normal,
        char_back,
        around_inverse,
        axial_inverse,
        normal_inverse,
    )
    right_side, update = -0.5 * right_side, update * active
    return right_side.reshape(conserved.shape), update.reshape(conserved.shape)


def solution(mesh):
    slabs = P(None, "ja", "ka", None)
    return jax.shard_map(
        body,
        mesh=mesh,
        in_specs=(slabs, P("ja", "ka", None), P("ja", None)) + (P(),) * 7,
        out_specs=(slabs, slabs),
        check_vma=False,
    )
```
